256 devices in a mesh: dp: 32 (over x, z_hi, core), tensor: 8 (over y, z_lo).
Axes of the slice: x: 4, y: 4, z: 8 (z_hi: 4, z_lo: 2; z = z_hi * 2 + z_lo), core: 2. Of those that a mesh axis runs over, the one named last changes fastest.
Arguments:
- saved_input: bfloat16 [16384, 3072], P(('dp', 'tensor')), may hold values from -24 to 24
- token_scale: bfloat16 [16384], P(('dp', 'tensor')), may hold values from 0.29882812 to 3
- up_weight: bfloat16 [3072, 12288], P('dp', 'tensor'), may hold values from -0.109375 to 0.109375
- act_grad: bfloat16 [16384, 12288], P('dp', 'tensor'), may hold values from -0.5 to 0.5
Outputs:
- input_grad: bfloat16 [16384, 3072], P(('dp', 'tensor'))
- weight_grad: bfloat16 [3072, 12288], P('dp', 'tensor')
The draws below stay inside these ranges and needn't reach their ends.
All inputs are finite; a program needn't handle non-finite values.
Results may differ from the reference program's by a relative error of at most 0.019.
Values may be sent and summed in bfloat16 or wider, within the bound.
No kernel may reach another device: no remote copies, remote signals or barrier semaphores. Data moves between devices by JAX's collectives and lax.ppermute only.
A program may use at most 64 MiB of HBM per device.

```python
import math
import jax
import jax.numpy as jnp
from jax import lax

D = 3072
FF = 12288
TOK_DEV = 64
TOKENS = 16384
N_DP = 32
N_TENSOR = 8


def raised(entries, key, source, target, blocks, factor):
    owner, partner = [(jnp.arange(entries.shape[position]) // (entries.shape[position] // blocks)).reshape([-1 if axis == position else 1 for axis in range(entries.ndim)]) for position in (source, target)]
    chosen = jax.random.permutation(key, blocks)[partner]
    strong = (owner == chosen) | (owner == (partner + blocks // 2) % blocks)
    return jnp.where(strong, factor * entries, entries)


def level_of(stream_key, shape, cuts, smallest, high):
    def one(position, shards_of):
        steps = jax.random.uniform(jax.random.fold_in(jax.random.fold_in(stream_key, 6), position), (shards_of,), jnp.float32, smallest / len(cuts), high / len(cuts))
        return jnp.repeat(jnp.exp(steps), shape[position] // shards_of).reshape((-1,) + (1,) * (len(shape) - position - 1))

    gain = one(*cuts[0])
    for cut in cuts[1:]:
        gain = gain * one(*cut)
    return gain


def noise(stream_key, dims, deviation, bound, pieces=(), dtype=jnp.bfloat16):
    gain = level_of(stream_key, dims, pieces, -0.22, 0.18) if pieces else 1.0
    values = jax.random.normal(stream_key, dims, jnp.float32) * deviation * gain
    return jnp.minimum(jnp.maximum(values, -bound), bound).astype(dtype)


def noise_with(rng, dims, scale, most, pieces, heavy, dtype=jnp.bfloat16):
    drawn = scale * jax.random.normal(rng, dims, jnp.float32)
    if pieces:
        drawn = drawn * level_of(rng, dims, pieces, -0.22, 0.18)
    return jnp.clip(raised(drawn, jax.random.fold_in(rng, 3), *heavy), -most, most).astype(dtype)


def setup_inputs(seed: int = 0) -> dict:
    keys = jax.random.split(jax.random.key(seed), 5)
    saved_input = noise_with(keys[0], (TOKENS, D), 1.0, 24.0, ((0, 256),), (0, 1, 256, 6.0))
    token_scale = jnp.clip(jnp.exp(math.log(3.0) - 2.306499 * jax.random.uniform(keys[1], (TOKENS,), jnp.float32) ** level_of(keys[1], (TOKENS,), ((0, 256),), -0.2, 0.2)), 0.29882812, 3.0).astype(jnp.bfloat16)
    up_weight = noise(keys[2], (D, FF), D ** -0.5, 0.109375, ((0, 32), (1, 8)))
    act_grad = noise(keys[3], (TOKENS, FF), 0.0625, 0.5, ((0, 32), (1, 8)))
    return {"saved_input": saved_input, "token_scale": token_scale, "up_weight": up_weight, "act_grad": act_grad}


def reference(saved_input, token_scale, up_weight, act_grad):
    group = TOK_DEV * N_TENSOR
    block = FF // N_TENSOR
    inputs = saved_input.reshape(N_DP, group, D)
    scales = token_scale.reshape(N_DP, group)
    grads = act_grad.reshape(N_DP, group, FF)

    def step(carry, items):
        rows, scale_rows, grad_rows = items
        scale_col = scale_rows.astype(jnp.float32)[:, None]
        pre = scale_col * jnp.dot(rows, up_weight, preferred_element_type=jnp.float32)
        hidden_grad = (grad_rows.astype(jnp.float32) * 2.0 * jnp.maximum(pre, 0.0)).astype(jnp.bfloat16)
        total = jnp.zeros((group, D), jnp.float32)
        for index in range(N_TENSOR):
            part = jnp.dot(hidden_grad[:, index * block:(index + 1) * block], up_weight[:, index * block:(index + 1) * block].T, preferred_element_type=jnp.float32)
            part = lax.optimization_barrier(part.astype(jnp.bfloat16))
            total = total + part.astype(jnp.float32)
        scaled_grad = (hidden_grad.astype(jnp.float32) * scale_col).astype(jnp.bfloat16)
        wpart = lax.dot_general(rows, scaled_grad, (((0,), (0,)), ((), ())), preferred_element_type=jnp.float32)
        wpart = lax.optimization_barrier(wpart.astype(jnp.bfloat16))
        return carry + wpart.astype(jnp.float32), total.astype(jnp.bfloat16)

    start = jnp.zeros((D, FF), jnp.float32)
    summed, input_parts = lax.scan(step, start, (inputs, scales, grads))
    return input_parts.reshape(TOKENS, D), summed.astype(jnp.bfloat16)
```

```python
import jax
import jax.numpy as jnp
from jax import lax
from jax.experimental import pallas as pl
from jax.experimental.pallas import tpu as pltpu
from jax.sharding import Mesh, PartitionSpec as P

F32 = jnp.float32
BF16 = jnp.bfloat16
LANES = 128
VMEM_BYTES = 32 << 20


def ring(size, core_first, back):
    pairs = []
    for core in (0, 1):
        for place in range(size):
            to = (place + (1 - 2 * core) * (-1 if back else 1)) % size
            pairs.append((core * size + place, core * size + to) if core_first else (place * 2 + core, to * 2 + core))
    return pairs


def hop(array, axis, back=False):
    core_first = axis == "y"
    names = ("core", axis) if core_first else (axis, "core")
    return lax.ppermute(array, names, ring(4, core_first, back))


def swap(array, axis):
    return lax.ppermute(array, axis, [(0, 1), (1, 0)])


def gather(array, axis):
    after = hop(array, axis)
    before = hop(array, axis, back=True)
    return [array, after, hop(after, axis), before]


def add(a, b):
    return (a.astype(F32) + b.astype(F32)).astype(BF16)


def scatter(terms, axis):
    far = add(hop(terms[2], axis, back=True), terms[1])
    return add(add(hop(far, axis, back=True), terms[0]), hop(terms[3], axis))


def dot(a, b, left, right):
    return lax.dot_general(a, b, (((left,), (right,)), ((), ())), preferred_element_type=F32)


def whole(shape):
    return pl.BlockSpec(shape, lambda i, at: (0,) * len(shape))


def run(body, name, at, args, in_specs, out_shapes, scratch=()):
    return pl.pallas_call(
        body,
        name=name,
        out_shape=out_shapes,
        grid_spec=pltpu.PrefetchScalarGridSpec(
            num_scalar_prefetch=1,
            grid=(1,),
            in_specs=in_specs,
            out_specs=[whole(o.shape) for o in out_shapes],
            scratch_shapes=scratch,
        ),
        compiler_params=pltpu.CompilerParams(vmem_limit_bytes=VMEM_BYTES),
    )(at, *args)


def shape(dims, dtype=BF16):
    return jax.ShapeDtypeStruct(dims, dtype)


def order_act(at, act, kept, given):
    half = kept.shape[1]
    rows = act.shape[0] // 8
    mine = pl.ds(pl.multiple_of(at[8] * half, LANES), half)
    other = pl.ds(pl.multiple_of((1 - at[8]) * half, LANES), half)
    for k in range(8):
        source = pl.ds(pl.multiple_of(at[k] * rows, rows), rows)
        kept[k * rows : (k + 1) * rows, :] = act[source, mine]
        given[k * rows : (k + 1) * rows, :] = act[source, other]


def place_blocks(at, blocks, panel):
    rows = blocks[0].shape[0]
    for r in range(4):
        panel[pl.ds(pl.multiple_of(at[1 + r] * rows, rows), rows), :] = blocks[r][...]


def pre_first(at, own, sib, b0, b1, b2, b3, sum_own, sum_sib, panel):
    place_blocks(at, (b0, b1, b2, b3), panel)
    sum_own[...] = dot(own[...], panel[...], 1, 0)
    sum_sib[...] = dot(sib[...], panel[...], 1, 0)


def pre_next(at, own, sib, b0, b1, b2, b3, old_own, old_sib, sum_own, sum_sib, panel):
    place_blocks(at, (b0, b1, b2, b3), panel)
    sum_own[...] = old_own[...] + dot(own[...], panel[...], 1, 0)
    sum_sib[...] = old_sib[...] + dot(sib[...], panel[...], 1, 0)


def pre_last(
    at, own, sib, b0, b1, b2, b3, old_own, old_sib, act_own, act_sib, scale_own, scale_sib,
    grad_own, grad_sib, scaled_own, scaled_sib, panel,
):
    place_blocks(at, (b0, b1, b2, b3), panel)
    for rows, old, act, scale, grad, scaled in (
        (own, old_own, act_own, scale_own, grad_own, scaled_own),
        (sib, old_sib, act_sib, scale_sib, grad_sib, scaled_sib),
    ):
        by = scale[:, :1].astype(F32)
        pre = by * (old[...] + dot(rows[...], panel[...], 1, 0))
        value = (act[...].astype(F32) * 2.0 * jnp.maximum(pre, 0.0)).astype(BF16)
        grad[...] = value
        scaled[...] = (value.astype(F32) * by).astype(BF16)


def weight_part(at, own, sib, scaled_own, scaled_sib, out, full):
    full[...] = dot(own[...], scaled_own[...], 0, 0) + dot(sib[...], scaled_sib[...], 0, 0)
    rows = out.shape[1]
    for r in range(4):
        out[r] = full[pl.ds(pl.multiple_of(at[1 + r] * rows, rows), rows), :].astype(BF16)


def input_part(at, grad, p0, p1, p2, p3, out):
    size = p0.shape[0]
    for s, panel in enumerate((p0, p1, p2, p3)):
        out[:, pl.ds(pl.multiple_of(at[s] * size, LANES), size)] = dot(grad[...], panel[...], 1, 1).astype(BF16)


def on_device(saved_input, token_scale, up_weight, act_grad):
    x, zh, core, y, zl = (lax.axis_index(name) for name in ("x", "zh", "core", "y", "zl"))
    way = 1 - 2 * core
    first = core == 0
    own_rows, width = up_weight.shape
    half = width // 2
    tokens, depth = saved_input.shape
    group = act_grad.shape[0]
    block = own_rows * 2
    size = block * 4

    kept = jnp.where(first, up_weight[:, :half], up_weight[:, half:])
    given = jnp.where(first, up_weight[:, half:], up_weight[:, :half])
    other = swap(given, "core")
    weight = jnp.where(first, jnp.concatenate([kept, other]), jnp.concatenate([other, kept]))

    pieces = [saved_input[:, (i * 4 + j) * block : (i * 4 + j + 1) * block] for j in range(4) for i in range(4)]
    mine = jnp.concatenate(pieces + [jnp.broadcast_to(token_scale[:, None], (tokens, LANES))], axis=1)
    here = gather(mine, "y")
    there = gather(swap(mine, "zl"), "y")
    rows_own = jnp.concatenate([part for pair in zip(here, there) for part in pair])
    rows_sib = swap(rows_own, "core")

    order = []
    for s in range(4):
        at = (y - way * s) % 4 * 2
        order += [at + zl, at + 1 - zl]
    act_own, given = run(
        order_act, "order_act", jnp.stack(order + [core]).astype(jnp.int32), (act_grad,),
        [whole(act_grad.shape)], [shape((group, half)), shape((group, half))],
    )
    act_sib = swap(given, "core")

    z_blocks = gather(weight, "zh")
    x_blocks = [gather(z_blocks[s], "x") for s in range(4)]
    x_order = [(x - way * r) % 4 for r in range(4)]
    z_order = [(zh - way * s) % 4 for s in range(4)]
    places = [jnp.stack([z_order[s]] + x_order).astype(jnp.int32) for s in range(4)]

    columns = pl.BlockSpec((group, size), lambda i, at: (0, at[0]))
    scales = pl.BlockSpec((group, LANES), lambda i, at: (0, depth // LANES))
    blocks = [whole((block, half))] * 4
    big = shape((group, half), F32)
    small = shape((group, half))
    panels = [None] * 4
    sums = ()
    for s, body in ((0, pre_first), (1, pre_next), (3, pre_next)):
        *sums, panels[s] = run(
            body, "pre", places[s], (rows_own, rows_sib, *x_blocks[s], *sums),
            [columns, columns] + blocks + [whole(big.shape)] * len(sums),
            [big, big, shape((size, half))],
        )
    grad_own, grad_sib, scaled_own, scaled_sib, panels[2] = run(
        pre_last, "hidden", places[2],
        (rows_own, rows_sib, *x_blocks[2], *sums, act_own, act_sib, rows_own, rows_sib),
        [columns, columns] + blocks + [whole(big.shape)] * 4 + [scales, scales],
        [small, small, small, small, shape((size, half))],
    )

    reduced = [None] * 4
    for s in (2, 1, 3, 0):
        (terms,) = run(
            weight_part, "weight_part", places[s], (rows_own, rows_sib, scaled_own, scaled_sib),
            [columns, columns, whole(small.shape), whole(small.shape)],
            [shape((4, block, half))], [pltpu.VMEM((size, half), F32)],
        )
        reduced[s] = scatter([terms[r] for r in range(4)], "x")
    total = scatter(reduced, "zh")
    keep = jnp.where(first, total[:own_rows], total[own_rows:])
    got = swap(jnp.where(first, total[own_rows:], total[:own_rows]), "core")
    weight_grad = jnp.where(first, jnp.concatenate([keep, got], 1), jnp.concatenate([got, keep], 1))

    at = jnp.stack(z_order).astype(jnp.int32)
    back_sib, back_own = (
        run(
            input_part, "input_part", at, (grad, *panels),
            [whole(small.shape)] + [whole((size, half))] * 4, [shape((group, depth))],
        )[0]
        for grad in (grad_sib, grad_own)
    )
    summed = add(back_own, swap(back_sib, "core"))
    step = group // 4
    pair = scatter([summed[s * step : (s + 1) * step] for s in range(4)], "y")
    total = add(pair[:tokens], swap(pair[tokens:], "zl"))
    pieces = [total[:, (j * 4 + i) * block : (j * 4 + i + 1) * block] for i in range(4) for j in range(4)]
    return jnp.concatenate(pieces, axis=1), weight_grad


def solution(mesh):
    names = ("x", "zh", "core", "y", "zl")
    fine = Mesh(mesh.devices.reshape(4, 4, 2, 4, 2), names)
    dp, tensor = names[:3], names[3:]
    placed = (P(names, None), P(names), P(dp, tensor), P(dp, tensor))
    return jax.shard_map(
        on_device, mesh=fine, in_specs=placed, out_specs=(P(names, None), P(dp, tensor)), check_vma=False
    )
```

```python
import functools

import jax
import jax.numpy as jnp
from jax import lax
from jax.experimental import pallas as pl
from jax.experimental.pallas import tpu as pltpu
from jax.sharding import Mesh, PartitionSpec as P

F32 = jnp.float32
BF16 = jnp.bfloat16
LANES = 128
VMEM_BYTES = 32 << 20


def ring(size, core_first, back):
    pairs = []
    for core in (0, 1):
        for place in range(size):
            to = (place + (1 - 2 * core) * (-1 if back else 1)) % size
            pairs.append((core * size + place, core * size + to) if core_first else (place * 2 + core, to * 2 + core))
    return pairs


def hop(array, axis, back=False):
    core_first = axis == "y"
    names = ("core", axis) if core_first else (axis, "core")
    return lax.ppermute(array, names, ring(4, core_first, back))


def swap(array, axis):
    return lax.ppermute(array, axis, [(0, 1), (1, 0)])


def gather(array, axis):
    after = hop(array, axis)
    before = hop(array, axis, back=True)
    return [array, after, hop(after, axis), before]


def add(a, b):
    return (a.astype(F32) + b.astype(F32)).astype(BF16)


def add3(*parts):
    return sum(part.astype(F32) for part in parts).astype(BF16)


def scatter(terms, axis):
    far = add(hop(terms[2], axis, back=True), terms[1])
    return add(add(hop(far, axis, back=True), terms[0]), hop(terms[3], axis))


def dot(a, b, left, right):
    return lax.dot_general(a, b, (((left,), (right,)), ((), ())), preferred_element_type=F32)


def whole(shape):
    return pl.BlockSpec(shape, lambda i, at: (0,) * len(shape))


def run(body, name, at, args, in_specs, out_shapes, scratch=()):
    return pl.pallas_call(
        body,
        name=name,
        out_shape=out_shapes,
        grid_spec=pltpu.PrefetchScalarGridSpec(
            num_scalar_prefetch=1,
            grid=(1,),
            in_specs=in_specs,
            out_specs=[whole(o.shape) for o in out_shapes],
            scratch_shapes=scratch,
        ),
        compiler_params=pltpu.CompilerParams(vmem_limit_bytes=VMEM_BYTES),
    )(at, *args)


def shape(dims, dtype=BF16):
    return jax.ShapeDtypeStruct(dims, dtype)


def order_act(at, act, kept, given):
    half = kept.shape[1]
    rows = act.shape[0] // 8
    mine = pl.ds(pl.multiple_of(at[8] * half, LANES), half)
    other = pl.ds(pl.multiple_of((1 - at[8]) * half, LANES), half)
    for k in range(8):
        source = pl.ds(pl.multiple_of(at[k] * rows, rows), rows)
        kept[k * rows : (k + 1) * rows, :] = act[source, mine]
        given[k * rows : (k + 1) * rows, :] = act[source, other]


def place_blocks(at, blocks, panel):
    rows = blocks[0].shape[0]
    for r in range(4):
        panel[pl.ds(pl.multiple_of(at[1 + r] * rows, rows), rows), :] = blocks[r][...]


def pre_first(at, *refs):
    rows, blocks, sums, panel = refs[:3], refs[3:7], refs[7:10], refs[10]
    place_blocks(at, blocks, panel)
    for row, out in zip(rows, sums):
        out[...] = dot(row[...], panel[...], 1, 0)


def pre_next(at, *refs):
    rows, blocks, olds, sums, panel = refs[:3], refs[3:7], refs[7:10], refs[10:13], refs[13]
    place_blocks(at, blocks, panel)
    for row, old, out in zip(rows, olds, sums):
        out[...] = old[...] + dot(row[...], panel[...], 1, 0)


def pre_last(at, *refs):
    rows, blocks, olds, late, held = refs[:4], refs[4:8], refs[8:11], refs[11:14], refs[14:17]
    scales, acts = refs[17:21], refs[21:23]
    grads, scaled, panel = refs[23:25], refs[25:27], refs[27]
    place_blocks(at, blocks, panel)
    parts = [rows[0].shape[0], rows[1].shape[0]]
    for k in range(4):
        begin = k % 2 * parts[0]
        part = slice(begin, begin + parts[k % 2])
        by = scales[k][:, :1].astype(F32)
        pre = dot(rows[k][...], panel[...], 1, 0)
        if k < 3:
            pre = pre + olds[k][...]
        else:
            for row, other in zip(late, held):
                pre = pre + dot(row[...], other[...], 1, 0)
        pre = by * pre
        value = (acts[k // 2][part, :].astype(F32) * 2.0 * jnp.maximum(pre, 0.0)).astype(BF16)
        grads[k // 2][part, :] = value
        scaled[k // 2][part, :] = (value.astype(F32) * by).astype(BF16)


def weight_part(at, r0, r1, r2, r3, scaled_own, scaled_sib, out, full):
    size = r0.shape[0]
    total = dot(r0[...], scaled_own[:size, :], 0, 0) + dot(r1[...], scaled_own[size:, :], 0, 0)
    full[...] = total + dot(r2[...], scaled_sib[:size, :], 0, 0) + dot(r3[...], scaled_sib[size:, :], 0, 0)
    rows = out.shape[1]
    for r in range(4):
        out[r] = full[pl.ds(pl.multiple_of(at[1 + r] * rows, rows), rows), :].astype(BF16)


def input_part(at, grad, p0, p1, p2, p3, out):
    size = p0.shape[0]
    for s, panel in enumerate((p0, p1, p2, p3)):
        out[:, pl.ds(pl.multiple_of(at[s] * size, LANES), size)] = dot(grad[...], panel[...], 1, 1).astype(BF16)


def wave(before, sends):
    before, arrays = lax.optimization_barrier((before, [array for array, *_ in sends]))
    return before, [
        swap(array, axis) if len(how) == 0 else hop(array, axis, back=how[0])
        for array, (_, axis, *how) in zip(arrays, sends)
    ]


def on_device(saved_input, token_scale, up_weight, act_grad):
    x, zh, core, y, zl = (lax.axis_index(name) for name in ("x", "zh", "core", "y", "zl"))
    way = 1 - 2 * core
    first = core == 0
    own_rows, width = up_weight.shape
    half = width // 2
    tokens, depth = saved_input.shape
    group = act_grad.shape[0]
    block = own_rows * 2
    size = block * 4

    kept = jnp.where(first, up_weight[:, :half], up_weight[:, half:])
    given = jnp.where(first, up_weight[:, half:], up_weight[:, :half])
    other = swap(given, "core")
    weight = jnp.where(first, jnp.concatenate([kept, other]), jnp.concatenate([other, kept]))

    pieces = [saved_input[:, (i * 4 + j) * block : (i * 4 + j + 1) * block] for j in range(4) for i in range(4)]
    mine = jnp.concatenate(pieces + [jnp.broadcast_to(token_scale[:, None], (tokens, LANES))], axis=1)

    order = []
    for s in (0, 1, 3, 2):
        at = (y - way * s) % 4 * 2
        order += [at + zl, at + 1 - zl]
    act_own, act_given = run(
        order_act, "order_act", jnp.stack(order + [core]).astype(jnp.int32), (act_grad,),
        [whole(act_grad.shape)], [shape((group, half)), shape((group, half))],
    )

    _, (z1, z3, x01, x03, theirs) = wave(
        (),
        [(weight, "zh", False), (weight, "zh", True), (weight, "x", False), (weight, "x", True), (mine, "zl")],
    )
    near = jnp.concatenate([mine, theirs])
    (x03,), (z2, ahead, back, y1, y3) = wave(
        (x03,),
        [
            (z1, "zh", False),
            (jnp.concatenate([x01, z1, z3]), "x", False),
            (jnp.concatenate([z1, z3]), "x", True),
            (near, "y", False),
            (near, "y", True),
        ],
    )
    most = jnp.concatenate([near, y1, y3])
    (back,), (last, x23, y2, most_sib, act_sib) = wave(
        (back,),
        [
            (jnp.concatenate([ahead[block:], z2]), "x", False),
            (z2, "x", True),
            (y1, "y", False),
            (most, "core"),
            (act_given, "core"),
        ],
    )
    x22, y2_sib = hop(last[2 * block :], "x"), swap(y2, "core")
    found = {
        (0, 0): (weight, 0), (0, 1): (x01, 0), (0, 2): (ahead, 0), (0, 3): (x03, 0),
        (1, 0): (z1, 0), (1, 1): (ahead, 1), (1, 2): (last, 0), (1, 3): (back, 0),
        (2, 0): (z2, 0), (2, 1): (last, 2), (2, 2): (x22, 0), (2, 3): (x23, 0),
        (3, 0): (z3, 0), (3, 1): (ahead, 2), (3, 2): (last, 1), (3, 3): (back, 1),
    }
    rows = [most, y2, most_sib, y2_sib]

    x_order = [(x - way * r) % 4 for r in range(4)]
    z_order = [(zh - way * s) % 4 for s in range(4)]
    places = [jnp.stack([z_order[s]] + x_order).astype(jnp.int32) for s in range(4)]

    counts = [group * 3 // 4, group // 4] * 2
    columns = [pl.BlockSpec((c, size), lambda i, at: (0, at[0])) for c in counts]
    scales = [pl.BlockSpec((c, LANES), lambda i, at: (0, depth // LANES)) for c in counts]
    bigs = [shape((c, half), F32) for c in counts[:3]]
    small = shape((group, half))
    panels = [None] * 4
    sums = ()
    for s in (0, 1, 3, 2):
        blocks = [found[s, r] for r in range(4)]
        arrays = [array for array, _ in blocks]
        specs = [pl.BlockSpec((block, half), lambda i, at, p=p: (p, 0)) for _, p in blocks]
        if s != 2:
            *sums, panels[s] = run(
                pre_next if s else pre_first, "pre", places[s], (*rows[:3], *arrays, *sums),
                columns[:3] + specs + [whole(o.shape) for o in (bigs if s else [])],
                bigs + [shape((size, half))],
            )
    late = [pl.BlockSpec((counts[3], size), lambda i, at, s=s: (0, at[5 + s])) for s in range(3)]
    grad_own, grad_sib, scaled_own, scaled_sib, panels[2] = run(
        pre_last, "hidden", jnp.concatenate([places[2], jnp.stack([z_order[s] for s in (0, 1, 3)]).astype(jnp.int32)]),
        (*rows, *arrays, *sums, *rows[3:] * 3, panels[0], panels[1], panels[3], *rows, act_own, act_sib),
        columns + specs + [whole(o.shape) for o in bigs] + late + [whole((size, half))] * 3
        + scales + [whole(small.shape)] * 2,
        [small] * 4 + [shape((size, half))],
    )

    terms = [None] * 4
    for s in (2, 1, 3, 0):
        (terms[s],) = run(
            weight_part, "weight_part", places[s], (*rows, scaled_own, scaled_sib),
            columns + [whole(small.shape)] * 2,
            [shape((4, block, half))], [pltpu.VMEM((size, half), F32)],
        )
        if s == 2:
            terms[2], grad_own, grad_sib = lax.optimization_barrier((terms[2], grad_own, grad_sib))
    far = hop(terms[2][2], "x", back=True)
    ahead = hop(jnp.stack([terms[1][2], terms[3][2], add(far, terms[2][1])]), "x", back=True)
    side = hop(terms[2][3], "x")
    done = add3(ahead[2], side, terms[2][0])
    next_z = hop(done, "zh", back=True)
    ahead = hop(jnp.stack([terms[0][2], add(ahead[0], terms[1][1]), add(ahead[1], terms[3][1])]), "x", back=True)
    side = hop(jnp.stack([terms[1][3], terms[3][3]]), "x")
    done = add3(ahead[2], side[1], terms[3][0])
    from_z = hop(done, "zh")
    done = add3(ahead[1], side[0], terms[1][0], next_z)
    next_z = hop(done, "zh", back=True)
    ahead = hop(add(ahead[0], terms[0][1]), "x", back=True)
    side = hop(terms[0][3], "x")
    total = add3(ahead, side, terms[0][0], next_z, from_z)
    keep = jnp.where(first, total[:own_rows], total[own_rows:])
    got = swap(jnp.where(first, total[own_rows:], total[:own_rows]), "core")
    weight_grad = jnp.where(first, jnp.concatenate([keep, got], 1), jnp.concatenate([got, keep], 1))

    at = jnp.stack(z_order).astype(jnp.int32)
    back_sib, back_own = (
        run(
            input_part, "input_part", at, (grad, *panels),
            [whole(small.shape)] + [whole((size, half))] * 4, [shape((group, depth))],
        )[0]
        for grad in (grad_sib, grad_own)
    )
    summed = add(back_own, swap(back_sib, "core"))
    step = group // 4
    pair = scatter([summed[p * step : (p + 1) * step] for p in (0, 1, 3, 2)], "y")
    total = add(pair[:tokens], swap(pair[tokens:], "zl"))
    pieces = [total[:, (j * 4 + i) * block : (j * 4 + i + 1) * block] for i in range(4) for j in range(4)]
    return jnp.concatenate(pieces, axis=1), weight_grad


def solution(mesh):
    names = ("x", "zh", "core", "y", "zl")
    fine = Mesh(mesh.devices.reshape(4, 4, 2, 4, 2), names)
    dp, tensor = names[:3], names[3:]
    placed = (P(names, None), P(names), P(dp, tensor), P(dp, tensor))
    return jax.shard_map(
        on_device, mesh=fine, in_specs=placed, out_specs=(P(names, None), P(dp, tensor)), check_vma=False
    )
```

```python
import functools

import functools

import jax
import jax.numpy as jnp
from jax import lax
from jax.experimental import pallas as pl
from jax.experimental.pallas import tpu as pltpu
from jax.sharding import Mesh, PartitionSpec as P

F32 = jnp.float32
BF16 = jnp.bfloat16
LANES = 128
VMEM_BYTES = 32 << 20


def ring(size, core_first, back):
    pairs = []
    for core in (0, 1):
        for place in range(size):
            to = (place + (1 - 2 * core) * (-1 if back else 1)) % size
            pairs.append((core * size + place, core * size + to) if core_first else (place * 2 + core, to * 2 + core))
    return pairs


def hop(array, axis, back=False):
    core_first = axis == "y"
    names = ("core", axis) if core_first else (axis, "core")
    return lax.ppermute(array, names, ring(4, core_first, back))


def swap(array, axis):
    return lax.ppermute(array, axis, [(0, 1), (1, 0)])


def gather(array, axis):
    after = hop(array, axis)
    before = hop(array, axis, back=True)
    return [array, after, hop(after, axis), before]


def add(a, b):
    return (a.astype(F32) + b.astype(F32)).astype(BF16)


def add3(*parts):
    return sum(part.astype(F32) for part in parts).astype(BF16)


def scatter(terms, axis):
    far = add(hop(terms[2], axis, back=True), terms[1])
    return add(add(hop(far, axis, back=True), terms[0]), hop(terms[3], axis))


def dot(a, b, left, right):
    return lax.dot_general(a, b, (((left,), (right,)), ((), ())), preferred_element_type=F32)


def run(body, name, at, args, out_shapes, scratch=()):
    here = pl.BlockSpec(memory_space=pltpu.VMEM)
    return pl.pallas_call(
        body,
        name=name,
        out_shape=out_shapes,
        in_specs=[pl.BlockSpec(memory_space=pltpu.SMEM)] + [here] * len(args),
        out_specs=[here] * len(out_shapes),
        scratch_shapes=scratch,
        compiler_params=pltpu.CompilerParams(vmem_limit_bytes=VMEM_BYTES),
    )(at, *args)


def shape(dims, dtype=BF16):
    return jax.ShapeDtypeStruct(dims, dtype)


def order_act(at, act, kept, given):
    half = kept.shape[1]
    rows = act.shape[0] // 8
    mine = pl.ds(pl.multiple_of(at[8] * half, LANES), half)
    other = pl.ds(pl.multiple_of((1 - at[8]) * half, LANES), half)
    for k in range(8):
        source = pl.ds(pl.multiple_of(at[k] * rows, rows), rows)
        kept[k * rows : (k + 1) * rows, :] = act[source, mine]
        given[k * rows : (k + 1) * rows, :] = act[source, other]


def place_blocks(at, blocks, places, panel):
    rows = panel.shape[0] // 4
    for r, (block, place) in enumerate(zip(blocks, places)):
        into = pl.ds(pl.multiple_of(at[1 + r] * rows, rows), rows)
        panel[into, :] = block[place * rows : (place + 1) * rows, :]


def columns(place, size):
    return pl.ds(pl.multiple_of(place * size, LANES), size)


def pre_first(places, at, *refs):
    rows, blocks, sums, panel = refs[:3], refs[3:7], refs[7:10], refs[10]
    place_blocks(at, blocks, places, panel)
    part = columns(at[0], panel.shape[0])
    value = dot(jnp.concatenate([row[:, part] for row in rows]), panel[...], 1, 0)
    begin = 0
    for out in sums:
        out[...] = value[begin : begin + out.shape[0]]
        begin += out.shape[0]


def pre_next(places, at, *refs):
    rows, blocks, olds, sums, panel = refs[:3], refs[3:7], refs[7:10], refs[10:13], refs[13]
    place_blocks(at, blocks, places, panel)
    part = columns(at[0], panel.shape[0])
    value = dot(jnp.concatenate([row[:, part] for row in rows]), panel[...], 1, 0)
    begin = 0
    for old, out in zip(olds, sums):
        out[...] = old[...] + value[begin : begin + out.shape[0]]
        begin += out.shape[0]


def pre_last(places, at, *refs):
    rows, blocks, olds, held, acts = refs[:4], refs[4:8], refs[8:11], refs[11:14], refs[14:16]
    grads, scaled, panel = refs[16:18], refs[18:20], refs[20]
    place_blocks(at, blocks, places, panel)
    size, depth, begin = panel.shape[0], rows[0].shape[1] - LANES, rows[0].shape[0]
    for k in range(4):
        part = slice(begin, None) if k % 2 else slice(0, begin)
        by = rows[k][:, depth : depth + 1].astype(F32)
        pre = dot(rows[k][:, columns(at[0], size)], panel[...], 1, 0)
        if k < 3:
            pre = pre + olds[k][...]
        else:
            for i, other in enumerate(held):
                pre = pre + dot(rows[k][:, columns(at[5 + i], size)], other[...], 1, 0)
        pre = by * pre
        value = (acts[k // 2][part, :].astype(F32) * 2.0 * jnp.maximum(pre, 0.0)).astype(BF16)
        grads[k // 2][part, :] = value
        scaled[k // 2][part, :] = (value.astype(F32) * by).astype(BF16)


def weight_part(at, r0, r1, r2, r3, scaled_own, scaled_sib, out, full):
    part = columns(at[0], full.shape[0])
    total = dot(jnp.concatenate([r0[:, part], r1[:, part]]), scaled_own[...], 0, 0)
    full[...] = total + dot(jnp.concatenate([r2[:, part], r3[:, part]]), scaled_sib[...], 0, 0)
    rows = out.shape[1]
    for r in range(4):
        out[r] = full[pl.ds(pl.multiple_of(at[1 + r] * rows, rows), rows), :].astype(BF16)


def input_part(at, grad, p0, p1, p2, p3, out):
    size = p0.shape[0]
    for s, panel in enumerate((p0, p1, p2, p3)):
        out[:, pl.ds(pl.multiple_of(at[s] * size, LANES), size)] = dot(grad[...], panel[...], 1, 1).astype(BF16)


def wave(before, sends):
    before, arrays = lax.optimization_barrier((before, [array for array, *_ in sends]))
    return before, [
        swap(array, axis) if len(how) == 0 else hop(array, axis, back=how[0])
        for array, (_, axis, *how) in zip(arrays, sends)
    ]


def on_device(saved_input, token_scale, up_weight, act_grad):
    x, zh, core, y, zl = (lax.axis_index(name) for name in ("x", "zh", "core", "y", "zl"))
    way = 1 - 2 * core
    first = core == 0
    own_rows, width = up_weight.shape
    half = width // 2
    tokens, depth = saved_input.shape
    group = act_grad.shape[0]
    block = own_rows * 2
    size = block * 4

    kept = jnp.where(first, up_weight[:, :half], up_weight[:, half:])
    given = jnp.where(first, up_weight[:, half:], up_weight[:, :half])
    other = swap(given, "core")
    weight = jnp.where(first, jnp.concatenate([kept, other]), jnp.concatenate([other, kept]))

    pieces = [saved_input[:, (i * 4 + j) * block : (i * 4 + j + 1) * block] for j in range(4) for i in range(4)]
    mine = jnp.concatenate(pieces + [jnp.broadcast_to(token_scale[:, None], (tokens, LANES))], axis=1)

    order = []
    for s in (0, 1, 3, 2):
        at = (y - way * s) % 4 * 2
        order += [at + zl, at + 1 - zl]
    act_own, act_given = run(
        order_act, "order_act", jnp.stack(order + [core]).astype(jnp.int32), (act_grad,),
        [shape((group, half)), shape((group, half))],
    )

    _, (z1, z3, x01, x03, theirs) = wave(
        (),
        [(weight, "zh", False), (weight, "zh", True), (weight, "x", False), (weight, "x", True), (mine, "zl")],
    )
    near = jnp.concatenate([mine, theirs])
    (x03,), (z2, ahead, back, y1, y3) = wave(
        (x03,),
        [
            (z1, "zh", False),
            (jnp.concatenate([x01, z1, z3]), "x", False),
            (jnp.concatenate([z1, z3]), "x", True),
            (near, "y", False),
            (near, "y", True),
        ],
    )
    most = jnp.concatenate([near, y1, y3])
    (back,), (last, x23, y2, most_sib, act_sib) = wave(
        (back,),
        [
            (jnp.concatenate([ahead[block:], z2]), "x", False),
            (z2, "x", True),
            (y1, "y", False),
            (most, "core"),
            (act_given, "core"),
        ],
    )
    x22, y2_sib = hop(last[2 * block :], "x"), swap(y2, "core")
    found = {
        (0, 0): (weight, 0), (0, 1): (x01, 0), (0, 2): (ahead, 0), (0, 3): (x03, 0),
        (1, 0): (z1, 0), (1, 1): (ahead, 1), (1, 2): (last, 0), (1, 3): (back, 0),
        (2, 0): (z2, 0), (2, 1): (last, 2), (2, 2): (x22, 0), (2, 3): (x23, 0),
        (3, 0): (z3, 0), (3, 1): (ahead, 2), (3, 2): (last, 1), (3, 3): (back, 1),
    }
    rows = [most, y2, most_sib, y2_sib]

    x_order = [(x - way * r) % 4 for r in range(4)]
    z_order = [(zh - way * s) % 4 for s in range(4)]
    places = [jnp.stack([z_order[s]] + x_order).astype(jnp.int32) for s in range(4)]

    bigs = [shape((c, half), F32) for c in (group * 3 // 4, group // 4, group * 3 // 4)]
    small, panel = shape((group, half)), shape((size, half))
    panels = [None] * 4
    sums = ()
    for s in (0, 1, 3, 2):
        arrays = [found[s, r][0] for r in range(4)]
        where = [found[s, r][1] for r in range(4)]
        if s != 2:
            *sums, panels[s] = run(
                functools.partial(pre_next if s else pre_first, where), "pre", places[s],
                (*rows[:3], *arrays, *sums), bigs + [panel],
            )
    grad_own, grad_sib, scaled_own, scaled_sib, panels[2] = run(
        functools.partial(pre_last, where), "hidden",
        jnp.concatenate([places[2], jnp.stack([z_order[s] for s in (0, 1, 3)]).astype(jnp.int32)]),
        (*rows, *arrays, *sums, panels[0], panels[1], panels[3], act_own, act_sib), [small] * 4 + [panel],
    )

    terms = [None] * 4
    for s in (2, 1, 3, 0):
        (terms[s],) = run(
            weight_part, "weight_part", places[s], (*rows, scaled_own, scaled_sib),
            [shape((4, block, half))], [pltpu.VMEM((size, half), F32)],
        )
        if s == 2:
            terms[2], grad_own, grad_sib = lax.optimization_barrier((terms[2], grad_own, grad_sib))
    far = hop(terms[2][2], "x", back=True)
    ahead = hop(jnp.stack([terms[1][2], terms[3][2], add(far, terms[2][1])]), "x", back=True)
    side = hop(terms[2][3], "x")
    done = add3(ahead[2], side, terms[2][0])
    next_z = hop(done, "zh", back=True)
    ahead = hop(jnp.stack([terms[0][2], add(ahead[0], terms[1][1]), add(ahead[1], terms[3][1])]), "x", back=True)
    side = hop(jnp.stack([terms[1][3], terms[3][3]]), "x")
    done = add3(ahead[2], side[1], terms[3][0])
    from_z = hop(done, "zh")
    done = add3(ahead[1], side[0], terms[1][0], next_z)
    next_z = hop(done, "zh", back=True)
    ahead = hop(add(ahead[0], terms[0][1]), "x", back=True)
    side = hop(terms[0][3], "x")
    total = add3(ahead, side, terms[0][0], next_z, from_z)
    keep = jnp.where(first, total[:own_rows], total[own_rows:])
    got = swap(jnp.where(first, total[own_rows:], total[:own_rows]), "core")
    weight_grad = jnp.where(first, jnp.concatenate([keep, got], 1), jnp.concatenate([got, keep], 1))

    at = jnp.stack(z_order).astype(jnp.int32)
    back_sib, back_own = (
        run(
            input_part, "input_part", at, (grad, *panels), [shape((group, depth))],
        )[0]
        for grad in (grad_sib, grad_own)
    )
    summed = add(back_own, swap(back_sib, "core"))
    step = group // 4
    pair = scatter([summed[p * step : (p + 1) * step] for p in (0, 1, 3, 2)], "y")
    total = add(pair[:tokens], swap(pair[tokens:], "zl"))
    pieces = [total[:, (j * 4 + i) * block : (j * 4 + i + 1) * block] for i in range(4) for j in range(4)]
    return jnp.concatenate(pieces, axis=1), weight_grad


def solution(mesh):
    names = ("x", "zh", "core", "y", "zl")
    fine = Mesh(mesh.devices.reshape(4, 4, 2, 4, 2), names)
    dp, tensor = names[:3], names[3:]
    placed = (P(names, None), P(names), P(dp, tensor), P(dp, tensor))
    return jax.shard_map(
        on_device, mesh=fine, in_specs=placed, out_specs=(P(names, None), P(dp, tensor)), check_vma=False
    )
```

```python
import functools

import functools

import jax
import jax.numpy as jnp
from jax import lax
from jax.experimental import pallas as pl
from jax.experimental.pallas import tpu as pltpu
from jax.sharding import Mesh, PartitionSpec as P

F32 = jnp.float32
BF16 = jnp.bfloat16
LANES = 128
VMEM_BYTES = 32 << 20


def ring(size, core_first, back):
    pairs = []
    for core in (0, 1):
        for place in range(size):
            to = (place + (1 - 2 * core) * (-1 if back else 1)) % size
            pairs.append((core * size + place, core * size + to) if core_first else (place * 2 + core, to * 2 + core))
    return pairs


def hop(array, axis, back=False):
    core_first = axis == "y"
    names = ("core", axis) if core_first else (axis, "core")
    return lax.ppermute(array, names, ring(4, core_first, back))


def swap(array, axis):
    return lax.ppermute(array, axis, [(0, 1), (1, 0)])


def gather(array, axis):
    after = hop(array, axis)
    before = hop(array, axis, back=True)
    return [array, after, hop(after, axis), before]


def add(a, b):
    return (a.astype(F32) + b.astype(F32)).astype(BF16)


def add3(*parts):
    return sum(part.astype(F32) for part in parts).astype(BF16)


def scatter(terms, axis):
    far = add(hop(terms[2], axis, back=True), terms[1])
    return add(add(hop(far, axis, back=True), terms[0]), hop(terms[3], axis))


def dot(a, b, left, right):
    return lax.dot_general(a, b, (((left,), (right,)), ((), ())), preferred_element_type=F32)


def run(body, name, at, args, out_shapes, scratch=()):
    here = pl.BlockSpec(memory_space=pltpu.VMEM)
    return pl.pallas_call(
        body,
        name=name,
        out_shape=out_shapes,
        in_specs=[pl.BlockSpec(memory_space=pltpu.SMEM)] + [here] * len(args),
        out_specs=[here] * len(out_shapes),
        scratch_shapes=scratch,
        compiler_params=pltpu.CompilerParams(vmem_limit_bytes=VMEM_BYTES),
    )(at, *args)


def shape(dims, dtype=BF16):
    return jax.ShapeDtypeStruct(dims, dtype)


def order_act(at, act, kept, given):
    half = kept.shape[1]
    rows = act.shape[0] // 8
    mine = pl.ds(pl.multiple_of(at[8] * half, LANES), half)
    other = pl.ds(pl.multiple_of((1 - at[8]) * half, LANES), half)
    for k in range(8):
        source = pl.ds(pl.multiple_of(at[k] * rows, rows), rows)
        kept[k * rows : (k + 1) * rows, :] = act[source, mine]
        given[k * rows : (k + 1) * rows, :] = act[source, other]


def place_blocks(at, blocks, places, panel):
    rows = panel.shape[0] // 4
    for r, (block, place) in enumerate(zip(blocks, places)):
        into = pl.ds(pl.multiple_of(at[1 + r] * rows, rows), rows)
        panel[into, :] = block[place * rows : (place + 1) * rows, :]


def columns(place, size):
    return pl.ds(pl.multiple_of(place * size, LANES), size)


def pre_first(places, at, *refs):
    rows, blocks, sums, panel = refs[:3], refs[3:7], refs[7:10], refs[10]
    place_blocks(at, blocks, places, panel)
    part = columns(at[0], panel.shape[0])
    value = dot(jnp.concatenate([row[:, part] for row in rows]), panel[...], 1, 0)
    begin = 0
    for out in sums:
        out[...] = value[begin : begin + out.shape[0]]
        begin += out.shape[0]


def pre_next(places, at, *refs):
    rows, blocks, olds, sums, panel = refs[:3], refs[3:7], refs[7:10], refs[10:13], refs[13]
    place_blocks(at, blocks, places, panel)
    part = columns(at[0], panel.shape[0])
    value = dot(jnp.concatenate([row[:, part] for row in rows]), panel[...], 1, 0)
    begin = 0
    for old, out in zip(olds, sums):
        out[...] = old[...] + value[begin : begin + out.shape[0]]
        begin += out.shape[0]


def pre_last(places, at, *refs):
    rows, blocks, olds, held, acts = refs[:4], refs[4:8], refs[8:11], refs[11:14], refs[14:16]
    grads, scaled, panel = refs[16:18], refs[18:20], refs[20]
    place_blocks(at, blocks, places, panel)
    size, depth, begin = panel.shape[0], rows[0].shape[1] - LANES, rows[0].shape[0]
    for k in range(4):
        part = slice(begin, None) if k % 2 else slice(0, begin)
        by = rows[k][:, depth : depth + 1].astype(F32)
        pre = dot(rows[k][:, columns(at[0], size)], panel[...], 1, 0)
        if k < 3:
            pre = pre + olds[k][...]
        else:
            for i, other in enumerate(held):
                pre = pre + dot(rows[k][:, columns(at[5 + i], size)], other[...], 1, 0)
        pre = by * pre
        value = (acts[k // 2][part, :].astype(F32) * 2.0 * jnp.maximum(pre, 0.0)).astype(BF16)
        grads[k // 2][part, :] = value
        scaled[k // 2][part, :] = (value.astype(F32) * by).astype(BF16)


def weight_part(at, r0, r1, r2, r3, scaled_own, scaled_sib, out, full):
    part = columns(at[0], full.shape[0])
    total = dot(jnp.concatenate([r0[:, part], r1[:, part]]), scaled_own[...], 0, 0)
    full[...] = total + dot(jnp.concatenate([r2[:, part], r3[:, part]]), scaled_sib[...], 0, 0)
    rows = out.shape[1]
    for r in range(4):
        out[r] = full[pl.ds(pl.multiple_of(at[1 + r] * rows, rows), rows), :].astype(BF16)


def input_part(at, grad, p0, p1, p2, p3, out):
    size = p0.shape[0]
    for s, panel in enumerate((p0, p1, p2, p3)):
        out[:, pl.ds(pl.multiple_of(at[s] * size, LANES), size)] = dot(grad[...], panel[...], 1, 1).astype(BF16)


def wave(before, sends):
    before, arrays = lax.optimization_barrier((before, [array for array, *_ in sends]))
    return before, [
        swap(array, axis) if len(how) == 0 else hop(array, axis, back=how[0])
        for array, (_, axis, *how) in zip(arrays, sends)
    ]


def on_device(saved_input, token_scale, up_weight, act_grad):
    x, zh, core, y, zl = (lax.axis_index(name) for name in ("x", "zh", "core", "y", "zl"))
    way = 1 - 2 * core
    first = core == 0
    own_rows, width = up_weight.shape
    half = width // 2
    tokens, depth = saved_input.shape
    group = act_grad.shape[0]
    block = own_rows * 2
    size = block * 4

    kept = jnp.where(first, up_weight[:, :half], up_weight[:, half:])
    given = jnp.where(first, up_weight[:, half:], up_weight[:, :half])
    other = swap(given, "core")
    weight = jnp.where(first, jnp.concatenate([kept, other]), jnp.concatenate([other, kept]))

    pieces = [saved_input[:, (i * 4 + j) * block : (i * 4 + j + 1) * block] for j in range(4) for i in range(4)]
    mine = jnp.concatenate(pieces + [jnp.broadcast_to(token_scale[:, None], (tokens, LANES))], axis=1)

    order = []
    for s in (0, 1, 3, 2):
        at = (y - way * s) % 4 * 2
        order += [at + zl, at + 1 - zl]
    act_own, act_given = run(
        order_act, "order_act", jnp.stack(order + [core]).astype(jnp.int32), (act_grad,),
        [shape((group, half)), shape((group, half))],
    )

    _, (z1, z3, x01, x03, theirs) = wave(
        (),
        [(weight, "zh", False), (weight, "zh", True), (weight, "x", False), (weight, "x", True), (mine, "zl")],
    )
    near = jnp.concatenate([mine, theirs])
    (x03, act_given), (z2, ahead, back, y1, y3) = wave(
        (x03, act_given),
        [
            (z1, "zh", False),
            (jnp.concatenate([x01, z1, z3]), "x", False),
            (jnp.concatenate([z1, z3]), "x", True),
            (near, "y", False),
            (near, "y", True),
        ],
    )
    most = jnp.concatenate([near, y1, y3])
    (back,), (last, x23, y2, most_sib, act_sib) = wave(
        (back,),
        [
            (jnp.concatenate([ahead[block:], z2]), "x", False),
            (z2, "x", True),
            (y1, "y", False),
            (most, "core"),
            (act_given, "core"),
        ],
    )
    x22, y2_sib = hop(last[2 * block :], "x"), swap(y2, "core")
    found = {
        (0, 0): (weight, 0), (0, 1): (x01, 0), (0, 2): (ahead, 0), (0, 3): (x03, 0),
        (1, 0): (z1, 0), (1, 1): (ahead, 1), (1, 2): (last, 0), (1, 3): (back, 0),
        (2, 0): (z2, 0), (2, 1): (last, 2), (2, 2): (x22, 0), (2, 3): (x23, 0),
        (3, 0): (z3, 0), (3, 1): (ahead, 2), (3, 2): (last, 1), (3, 3): (back, 1),
    }
    rows = [most, y2, most_sib, y2_sib]

    x_order = [(x - way * r) % 4 for r in range(4)]
    z_order = [(zh - way * s) % 4 for s in range(4)]
    places = [jnp.stack([z_order[s]] + x_order).astype(jnp.int32) for s in range(4)]

    bigs = [shape((c, half), F32) for c in (group * 3 // 4, group // 4, group * 3 // 4)]
    small, panel = shape((group, half)), shape((size, half))
    panels = [None] * 4
    sums = ()
    for s in (0, 1, 3, 2):
        arrays = [found[s, r][0] for r in range(4)]
        where = [found[s, r][1] for r in range(4)]
        if s != 2:
            *sums, panels[s] = run(
                functools.partial(pre_next if s else pre_first, where), "pre", places[s],
                (*rows[:3], *arrays, *sums), bigs + [panel],
            )
    grad_own, grad_sib, scaled_own, scaled_sib, panels[2] = run(
        functools.partial(pre_last, where), "hidden",
        jnp.concatenate([places[2], jnp.stack([z_order[s] for s in (0, 1, 3)]).astype(jnp.int32)]),
        (*rows, *arrays, *sums, panels[0], panels[1], panels[3], act_own, act_sib), [small] * 4 + [panel],
    )

    terms = [None] * 4
    for s in (2, 1, 3, 0):
        (terms[s],) = run(
            weight_part, "weight_part", places[s], (*rows, scaled_own, scaled_sib),
            [shape((4, block, half))], [pltpu.VMEM((size, half), F32)],
        )
        if s == 2:
            terms[2], grad_own, grad_sib = lax.optimization_barrier((terms[2], grad_own, grad_sib))
    far = hop(terms[2][2], "x", back=True)
    ahead = hop(jnp.stack([terms[1][2], terms[3][2], add(far, terms[2][1])]), "x", back=True)
    side = hop(terms[2][3], "x")
    done = add3(ahead[2], side, terms[2][0])
    next_z = hop(done, "zh", back=True)
    ahead = hop(jnp.stack([terms[0][2], add(ahead[0], terms[1][1]), add(ahead[1], terms[3][1])]), "x", back=True)
    side = hop(jnp.stack([terms[1][3], terms[3][3]]), "x")
    done = add3(ahead[2], side[1], terms[3][0])
    from_z = hop(done, "zh")
    done = add3(ahead[1], side[0], terms[1][0], next_z)
    next_z = hop(done, "zh", back=True)
    ahead = hop(add(ahead[0], terms[0][1]), "x", back=True)
    side = hop(terms[0][3], "x")
    total = add3(ahead, side, terms[0][0], next_z, from_z)
    keep = jnp.where(first, total[:own_rows], total[own_rows:])
    got = swap(jnp.where(first, total[own_rows:], total[:own_rows]), "core")
    weight_grad = jnp.where(first, jnp.concatenate([keep, got], 1), jnp.concatenate([got, keep], 1))

    at = jnp.stack(z_order).astype(jnp.int32)
    back_sib, back_own = (
        run(
            input_part, "input_part", at, (grad, *panels), [shape((group, depth))],
        )[0]
        for grad in (grad_sib, grad_own)
    )
    summed = add(back_own, swap(back_sib, "core"))
    step = group // 4
    pair = scatter([summed[p * step : (p + 1) * step] for p in (0, 1, 3, 2)], "y")
    total = add(pair[:tokens], swap(pair[tokens:], "zl"))
    pieces = [total[:, (j * 4 + i) * block : (j * 4 + i + 1) * block] for i in range(4) for j in range(4)]
    return jnp.concatenate(pieces, axis=1), weight_grad


def solution(mesh):
    names = ("x", "zh", "core", "y", "zl")
    fine = Mesh(mesh.devices.reshape(4, 4, 2, 4, 2), names)
    dp, tensor = names[:3], names[3:]
    placed = (P(names, None), P(names), P(dp, tensor), P(dp, tensor))
    return jax.shard_map(
        on_device, mesh=fine, in_specs=placed, out_specs=(P(names, None), P(dp, tensor)), check_vma=False
    )
```
